32 devices in a mesh: pole: 2 (over y), row: 4 (over z), col: 4 (over x, core).
Axes of the slice: x: 2, y: 2, z: 4, core: 2. Of those that a mesh axis runs over, the one named last changes fastest.
Arguments:
- root_inverse: float32 [8192, 4096], P(('pole', 'row'), 'col'), parts along dimension 0, as said below
- root_factor_one: float32 [8192, 1024], P(('pole', 'row'), 'col'), parts along dimension 0, may hold values from -0.09375 to 0.09375
- diag_inverse_one: float32 [8, 256, 256], P(('pole', 'col')), parts along dimension 0
- root_factor_two: float32 [8192, 2048], P(('pole', 'row'), 'col'), parts along dimension 0, may hold values from -0.09375 to 0.09375
- parent_factor: float32 [16, 256, 256], P(('pole', 'col')), parts along dimension 0, may hold values from -0.109375 to 0.109375
- diag_inverse_two: float32 [16, 256, 256], P(('pole', 'col')), parts along dimension 0
- root_mask_one: int32 [4, 16], replicated, may hold values from 0 to 1, as said below
- root_mask_two: int32 [8, 16], replicated, may hold values from 0 to 1, as said below
- parents: int32 [8], replicated, may hold values from 0 to 3, as said below
Outputs:
- inverse_one: float32 [8192, 1024], P(('pole', 'row'), 'col'), parts along dimension 0
- diag_one: float32 [8, 256, 256], P(('pole', 'col')), parts along dimension 0
- inverse_two: float32 [8192, 2048], P(('pole', 'row'), 'col'), parts along dimension 0
- parent_block: float32 [16, 256, 256], P(('pole', 'col')), parts along dimension 0
- diag_two: float32 [16, 256, 256], P(('pole', 'col')), parts along dimension 0
The draws below stay inside these ranges and needn't reach their ends.
There are 2 independent parts, one for each index of `pole`. The reference program is written for one: setup_inputs(seed, part) draws one part's arguments, and reference() takes and returns one part's arrays. A program takes and returns all parts, laid end to end along the dimension named above; an argument that names none is the same for every part. Nothing has to cross between parts.
Inputs may be any that keep to these rules, and one draw needn't show every extreme that they name: `root_inverse`: symmetric. `root_mask_one`: 1 where root supernode b belongs to the structure of level-one supernode k. `root_mask_two`: 1 only where the same root supernode is 1 for the parent parents[k] in root_mask_one. `parents`: every level-one supernode is the parent of at least one level-two supernode.
All inputs are finite; a program needn't handle non-finite values.
Results may differ from the reference program's by a relative error of at most 0.000073.
Values sent between devices are 32-bit elements; how exact they have to be, the bound alone decides.
A program may use at most 128 MiB of HBM per device.

```python
import math
import jax
import jax.numpy as jnp
from jax import lax

W = 256
RB = 16
RW = 4096
N1 = 4
N2 = 8


def symmetric(noise, diagonal, factor):
    order = noise.shape[-1]
    unit = jnp.eye(order, dtype=jnp.float32)
    return (noise + jnp.swapaxes(noise, -1, -2)) * factor + unit * diagonal[..., None, :]


def structure(key):
    keys = jax.random.split(key, 4)
    first = jax.random.permutation(keys[0], jnp.arange(N1, dtype=jnp.int32))
    extra = jax.random.randint(keys[1], (N2 - N1,), 0, N1, dtype=jnp.int32)
    parent_ids = jnp.concatenate([first, extra]).astype(jnp.int32)
    mask_one = (jax.random.randint(keys[2], (N1, RB), 0, 4, dtype=jnp.int32) > 0).astype(jnp.int32)
    keep = jax.random.randint(keys[3], (N2, RB), 0, 4, dtype=jnp.int32) > 0
    mask_two = (keep & (mask_one[parent_ids] > 0)).astype(jnp.int32)
    return (parent_ids, mask_one, mask_two)


def draw_root_inverse(key, part):
    key = jax.random.fold_in(key, 11)
    keys = jax.random.split(key, 2)
    noise = jax.random.normal(keys[0], (RW, RW), jnp.float32)
    diagonal = jax.random.uniform(keys[1], (RW,), jnp.float32, 1.0, 3.0)
    return symmetric(noise, diagonal, 0.3 / math.sqrt(RW))


def draw_diag_inverse_one(key, part):
    key = jax.random.fold_in(key, 12)
    keys = jax.random.split(key, 2)
    noise = jax.random.normal(keys[0], (N1, W, W), jnp.float32)
    diagonal = jax.random.uniform(keys[1], (N1, W), jnp.float32, 1.0, 3.0)
    return symmetric(noise, diagonal, 0.3 / math.sqrt(W))


def draw_diag_inverse_two(key, part):
    key = jax.random.fold_in(key, 13)
    keys = jax.random.split(key, 2)
    noise = jax.random.normal(keys[0], (N2, W, W), jnp.float32)
    diagonal = jax.random.uniform(keys[1], (N2, W), jnp.float32, 1.0, 3.0)
    return symmetric(noise, diagonal, 0.3 / math.sqrt(W))


def draw_root_mask_one(key, part):
    parent_ids, mask_one, mask_two = structure(key)
    return mask_one


def draw_root_mask_two(key, part):
    parent_ids, mask_one, mask_two = structure(key)
    return mask_two


def draw_parents(key, part):
    parent_ids, mask_one, mask_two = structure(key)
    return parent_ids


def shard_levels(rng, extent, shards, smallest, largest):
    factor_of = 1.0
    for axis_at, parts in shards:
        steps = jax.random.uniform(jax.random.fold_in(jax.random.fold_in(rng, 6), axis_at), (parts,), jnp.float32, smallest / len(shards), largest / len(shards))
        factor_of = factor_of * jnp.repeat(jnp.exp(steps), extent[axis_at] // parts).reshape((-1,) + (1,) * (len(extent) - 1 - axis_at))
    return factor_of


def scatter_about(key, extent, spread, bound, cuts=(), held_as=jnp.bfloat16):
    gain = shard_levels(key, extent, cuts, -0.22, 0.18) if cuts else 1.0
    array = jax.random.normal(key, extent, jnp.float32) * spread * gain
    return jnp.minimum(jnp.maximum(array, -bound), bound).astype(held_as)


def setup_inputs(seed: int = 0, part: int = 0) -> dict:
    key_list = jax.random.split(jax.random.key(seed), 10)
    part_keys = jax.random.split(jax.random.fold_in(key_list[9], part), 10)
    root_inverse = draw_root_inverse(jax.random.fold_in(jax.random.fold_in(key_list[9], part), 71), part)
    root_factor_one = scatter_about(part_keys[1], (RW, N1 * W), RW ** -0.5, 0.09375, ((0, 4), (1, 4)), jnp.float32)
    diag_inverse_one = draw_diag_inverse_one(jax.random.fold_in(jax.random.fold_in(key_list[9], part), 71), part)
    root_factor_two = scatter_about(part_keys[3], (RW, N2 * W), RW ** -0.5, 0.09375, ((0, 4), (1, 4)), jnp.float32)
    parent_factor = scatter_about(part_keys[4], (N2, W, W), (W * 11) ** -0.5, 0.109375, ((0, 4),), jnp.float32)
    diag_inverse_two = draw_diag_inverse_two(jax.random.fold_in(jax.random.fold_in(key_list[9], part), 71), part)
    root_mask_one = draw_root_mask_one(jax.random.fold_in(key_list[9], 71), part)
    root_mask_two = draw_root_mask_two(jax.random.fold_in(key_list[9], 71), part)
    parents = draw_parents(jax.random.fold_in(key_list[9], 71), part)
    return dict(root_inverse=root_inverse, root_factor_one=root_factor_one, diag_inverse_one=diag_inverse_one, root_factor_two=root_factor_two, parent_factor=parent_factor, diag_inverse_two=diag_inverse_two, root_mask_one=root_mask_one, root_mask_two=root_mask_two, parents=parents)


def expand_mask(mask):
    marks = mask.astype(jnp.float32).T
    return jnp.repeat(jnp.repeat(marks, W, axis=0), W, axis=1)


def reference(root_inverse, root_factor_one, diag_inverse_one, root_factor_two, parent_factor, diag_inverse_two, root_mask_one, root_mask_two, parents):
    highest = lax.Precision.HIGHEST
    mask_one = expand_mask(root_mask_one)
    factor_one = root_factor_one * mask_one
    inverse_one = -jnp.dot(root_inverse, factor_one, precision=highest) * mask_one
    split_factor = factor_one.reshape(RW, N1, W)
    split_inverse = inverse_one.reshape(RW, N1, W)
    diag_one = diag_inverse_one - jnp.einsum("ikw,ikv->kwv", split_factor, split_inverse, precision=highest)
    mask_two = expand_mask(root_mask_two)
    factor_two = (root_factor_two * mask_two).reshape(RW, N2, W)
    parent_cols = jnp.take(split_inverse, parents, axis=1)
    parent_diag = jnp.take(diag_one, parents, axis=0)
    cross_term = jnp.einsum("ikw,kwv->ikv", parent_cols, parent_factor, precision=highest)
    root_term = jnp.dot(root_inverse, factor_two.reshape(RW, N2 * W), precision=highest).reshape(RW, N2, W)
    inverse_two = -(root_term + cross_term) * mask_two.reshape(RW, N2, W)
    parent_block = -(jnp.einsum("ikw,ikv->kwv", parent_cols, factor_two, precision=highest) + jnp.einsum("kwv,kvx->kwx", parent_diag, parent_factor, precision=highest))
    diag_two = diag_inverse_two - jnp.einsum("ikw,ikv->kwv", factor_two, inverse_two, precision=highest) - jnp.einsum("kwv,kwx->kvx", parent_factor, parent_block, precision=highest)
    return inverse_one, diag_one, inverse_two.reshape(RW, N2 * W), parent_block, diag_two
```

```python
import functools

import jax
import jax.numpy as jnp
from jax import lax
from jax.experimental import pallas as pl
from jax.experimental.pallas import tpu as pltpu
from jax.sharding import PartitionSpec as P

HIGH = lax.Precision.HIGH


MESH = pl.DeviceIdType.MESH
CHUNKS = 4


def gather_kernel(
    rows_n, chips, a_ref, f_ref, panel, whole, f_send, f_recv, x_send, x_recv, s_send, s_recv, own
):
    row, col = lax.axis_index("row"), lax.axis_index("col")
    core, chip = lax.rem(col, 2), col // 2
    sibling = chip * 2 + 1 - core
    height, wide = a_ref.shape
    step = height // CHUNKS
    tall = f_ref.shape[0]

    barrier = pltpu.get_barrier_semaphore()
    for s in range(1, rows_n):
        pl.semaphore_signal(
            barrier, inc=1, device_id={"row": lax.rem(row + s, rows_n)}, device_id_type=MESH
        )
    for d in range(1, chips):
        other = lax.rem(chip + d, chips) * 2 + core
        pl.semaphore_signal(barrier, inc=1, device_id={"col": other}, device_id_type=MESH)
    pl.semaphore_signal(barrier, inc=1, device_id={"col": sibling}, device_id_type=MESH)
    pl.semaphore_wait(barrier, rows_n + chips - 1)

    def slot(c, ch):
        return panel.at[pl.ds(ch * step, step), pl.ds(pl.multiple_of(c * wide, wide), wide)]

    def across(d, ch):
        return pltpu.make_async_remote_copy(
            src_ref=a_ref.at[pl.ds(ch * step, step)],
            dst_ref=slot(col, ch),
            send_sem=x_send.at[d - 1, ch],
            recv_sem=x_recv.at[d - 1, ch],
            device_id={"col": lax.rem(chip + d, chips) * 2 + core},
            device_id_type=MESH,
        )

    def beside(d, ch):
        source = lax.rem(chip + chips - d, chips) * 2 + core
        src = a_ref.at[pl.ds(ch * step, step)] if d == 0 else slot(source, ch)
        return pltpu.make_async_remote_copy(
            src_ref=src,
            dst_ref=slot(source, ch),
            send_sem=s_send.at[d, ch],
            recv_sem=s_recv.at[d, ch],
            device_id={"col": sibling},
            device_id_type=MESH,
        )

    def place(r):
        return whole.at[pl.ds(pl.multiple_of(r * tall, tall), tall)]

    copies = []
    for ch in range(CHUNKS):
        for d in range(1, chips):
            c = across(d, ch)
            c.start()
            copies.append(c)
    sends = []
    for s in range(1, rows_n):
        c = pltpu.make_async_remote_copy(
            src_ref=f_ref,
            dst_ref=place(row),
            send_sem=f_send.at[s - 1],
            recv_sem=f_recv.at[s - 1],
            device_id={"row": lax.rem(row + s, rows_n)},
            device_id_type=MESH,
        )
        c.start()
        sends.append(c)
    local_f = pltpu.make_async_copy(f_ref, place(row), own.at[0])
    local_f.start()
    local_a = pltpu.make_async_copy(
        a_ref, panel.at[:, pl.ds(pl.multiple_of(col * wide, wide), wide)], own.at[1]
    )
    local_a.start()
    forwards = []
    for ch in range(CHUNKS):
        c = beside(0, ch)
        c.start()
        forwards.append(c)
    at = 0
    for ch in range(CHUNKS):
        for d in range(1, chips):
            copies[at].wait_recv()
            at += 1
            c = beside(d, ch)
            c.start()
            forwards.append(c)
    for c in copies:
        c.wait_send()
    for c in forwards:
        c.wait()
    for c in sends:
        c.wait()
    local_f.wait()
    local_a.wait()


def gather_first(a, f, rows_n, cols_n):
    chips = cols_n // 2
    dma = pltpu.SemaphoreType.DMA
    return pl.pallas_call(
        functools.partial(gather_kernel, rows_n, chips),
        out_shape=(
            jax.ShapeDtypeStruct((a.shape[0], cols_n * a.shape[1]), a.dtype),
            jax.ShapeDtypeStruct((rows_n * f.shape[0], f.shape[1]), f.dtype),
        ),
        in_specs=[pl.BlockSpec(memory_space=pl.ANY)] * 2,
        out_specs=(pl.BlockSpec(memory_space=pl.ANY),) * 2,
        scratch_shapes=[
            dma((rows_n - 1,)),
            dma((rows_n - 1,)),
            dma((chips - 1, CHUNKS)),
            dma((chips - 1, CHUNKS)),
            dma((chips, CHUNKS)),
            dma((chips, CHUNKS)),
            dma((2,)),
        ],
        compiler_params=pltpu.CompilerParams(collective_id=0, has_side_effects=True),
    )(a, f)


def permuted(block, count):
    return [
        lax.ppermute(block, "row", [(i, (i + shift) % count) for i in range(count)])
        for shift in range(1, count)
    ]


def assemble(whole, block, pieces, count, index, column):
    rows = block.shape[0]
    for shift, piece in enumerate([block] + pieces):
        owner = lax.rem(index + count - shift, count)
        whole = lax.dynamic_update_slice(whole, piece, (owner * rows, jnp.int32(column)))
    return whole


def on_device(
    root_inverse,
    root_factor_one,
    diag_inverse_one,
    root_factor_two,
    parent_factor,
    diag_inverse_two,
    root_mask_one,
    root_mask_two,
    parents,
    row_count,
    col_count,
):
    width = parent_factor.shape[1]
    local_rows = root_inverse.shape[0]
    per_one = diag_inverse_one.shape[0]
    per_two = diag_inverse_two.shape[0]
    row_index = lax.axis_index("row")
    col_index = lax.axis_index("col")
    blocks = local_rows // width

    def row_masks(mask, number):
        own = lax.dynamic_slice(mask, (col_index * number, row_index * blocks), (number, blocks))
        return jnp.repeat(own.T.astype(jnp.float32), width, axis=0)

    mask_one = row_masks(root_mask_one, per_one)
    mask_two = row_masks(root_mask_two, per_two)
    one = [
        root_factor_one[:, k * width : (k + 1) * width] * mask_one[:, k : k + 1]
        for k in range(per_one)
    ]
    two = [
        root_factor_two[:, k * width : (k + 1) * width] * mask_two[:, k : k + 1]
        for k in range(per_two)
    ]
    half = width // 2
    early = jnp.concatenate(one + [two[0][:, :half]], axis=1)
    panel, whole_early = gather_first(root_inverse, early, row_count, col_count)
    late = [two[0][:, half:]] + two[1:]
    panel, late = lax.optimization_barrier((panel, late))
    pieces = [permuted(f, row_count) for f in late]
    whole_one = [whole_early[:, k * width : (k + 1) * width] for k in range(per_one)]
    start = jnp.pad(whole_early[:, per_one * width :], ((0, 0), (0, half)))
    whole_two = [assemble(start, late[0], pieces[0], row_count, row_index, half)]

    def dot(a, b):
        return jnp.dot(a, b, precision=HIGH, preferred_element_type=jnp.float32)

    def dot_t(a, b):
        return lax.dot_general(
            a, b, (((0,), (0,)), ((), ())), precision=HIGH, preferred_element_type=jnp.float32
        )

    inv_one = [-dot(panel, whole_one[k]) * mask_one[:, k : k + 1] for k in range(per_one)]
    inverse_one = jnp.concatenate(inv_one, axis=1) if per_one > 1 else inv_one[0]
    diag_part = jnp.stack([dot_t(one[k], inv_one[k]) for k in range(per_one)])
    own_parents = lax.dynamic_slice_in_dim(parents, col_index * per_two, per_two, 0)
    all_inverse = lax.all_gather(inverse_one, "col", axis=0, tiled=False)

    parent_cols = []
    for k in range(per_two):
        p = own_parents[k]
        wide = lax.dynamic_index_in_dim(all_inverse, p // per_one, 0, keepdims=False)
        parent_cols.append(lax.dynamic_slice_in_dim(wide, (p % per_one) * width, width, 1))
    parent_part = jnp.stack([dot_t(parent_cols[k], two[k]) for k in range(per_two)])
    summed_one, summed_parent = lax.psum((diag_part, parent_part), "row")
    diag_one = diag_inverse_one - summed_one
    all_diag = lax.all_gather(diag_one, "col", axis=0, tiled=True)
    parent_block, inv_two, diag_two = [], [], []
    for k in range(per_two):
        parent_diag = lax.dynamic_index_in_dim(all_diag, own_parents[k], 0, keepdims=False)
        parent_block.append(-(summed_parent[k] + dot(parent_diag, parent_factor[k])))
        cross = dot(parent_cols[k], parent_factor[k])
        if k == 0:
            total = dot(panel, whole_two[0]) + cross
        else:
            total = cross
            for shift, piece in enumerate([late[k]] + pieces[k]):
                owner = lax.rem(row_index + row_count - shift, row_count)
                columns = lax.dynamic_slice_in_dim(panel, owner * local_rows, local_rows, 1)
                total = total + dot(columns, piece)
        inv_two.append(-total * mask_two[:, k : k + 1])
    diag_part_two = jnp.stack([dot_t(two[k], inv_two[k]) for k in range(per_two)])
    diag_part_two, parent_block = lax.optimization_barrier((diag_part_two, parent_block))
    summed_diag = lax.psum(diag_part_two, "row")
    diag_two = [
        diag_inverse_two[k] - summed_diag[k] - dot_t(parent_factor[k], parent_block[k])
        for k in range(per_two)
    ]
    return (
        inverse_one,
        diag_one,
        jnp.concatenate(inv_two, axis=1),
        jnp.stack(parent_block),
        jnp.stack(diag_two),
    )


def solution(mesh):
    row_count, col_count = mesh.shape["row"], mesh.shape["col"]
    tall = P(("pole", "row"), "col")
    deep = P(("pole", "col"), None, None)

    def step(*args):
        return on_device(*args, row_count, col_count)

    return jax.shard_map(
        step,
        mesh=mesh,
        in_specs=(tall, tall, deep, tall, deep, deep, P(), P(), P()),
        out_specs=(tall, deep, tall, deep, deep),
        check_vma=False,
    )
```

```python
import functools

import jax
import jax.numpy as jnp
from jax import lax
from jax.experimental import pallas as pl
from jax.experimental.pallas import tpu as pltpu
from jax.sharding import PartitionSpec as P

HIGH = lax.Precision.HIGH


MESH = pl.DeviceIdType.MESH


def gather_kernel(rows_n, f_ref, whole, f_send, f_recv, own):
    row = lax.axis_index("row")
    tall = f_ref.shape[0]
    barrier = pltpu.get_barrier_semaphore()
    for s in range(1, rows_n):
        pl.semaphore_signal(
            barrier, inc=1, device_id={"row": lax.rem(row + s, rows_n)}, device_id_type=MESH
        )
    pl.semaphore_wait(barrier, rows_n - 1)
    place = whole.at[pl.ds(pl.multiple_of(row * tall, tall), tall)]
    sends = []
    for s in range(1, rows_n):
        c = pltpu.make_async_remote_copy(
            src_ref=f_ref,
            dst_ref=place,
            send_sem=f_send.at[s - 1],
            recv_sem=f_recv.at[s - 1],
            device_id={"row": lax.rem(row + s, rows_n)},
            device_id_type=MESH,
        )
        c.start()
        sends.append(c)
    local = pltpu.make_async_copy(f_ref, place, own)
    local.start()
    for c in sends:
        c.wait()
    local.wait()


def gather_first(f, rows_n, number):
    dma = pltpu.SemaphoreType.DMA
    return pl.pallas_call(
        functools.partial(gather_kernel, rows_n),
        out_shape=jax.ShapeDtypeStruct((rows_n * f.shape[0], f.shape[1]), f.dtype),
        in_specs=[pl.BlockSpec(memory_space=pl.ANY)],
        out_specs=pl.BlockSpec(memory_space=pl.ANY),
        scratch_shapes=[dma((rows_n - 1,)), dma((rows_n - 1,)), dma],
        compiler_params=pltpu.CompilerParams(collective_id=number, has_side_effects=True),
    )(f)


def reduce_kernel(rows_n, x_ref, out_ref, inbox, a_send, a_recv, b_send, b_recv):
    row = lax.axis_index("row")
    part = x_ref.shape[0] // rows_n
    barrier = pltpu.get_barrier_semaphore()
    for s in range(1, rows_n):
        pl.semaphore_signal(
            barrier, inc=1, device_id={"row": lax.rem(row + s, rows_n)}, device_id_type=MESH
        )
    pl.semaphore_wait(barrier, rows_n - 1)

    def piece(r):
        return pl.ds(pl.multiple_of(r * part, part), part)

    sends = []
    for s in range(1, rows_n):
        other = lax.rem(row + s, rows_n)
        c = pltpu.make_async_remote_copy(
            src_ref=x_ref.at[piece(other)],
            dst_ref=inbox.at[s - 1],
            send_sem=a_send.at[s - 1],
            recv_sem=a_recv.at[s - 1],
            device_id={"row": other},
            device_id_type=MESH,
        )
        c.start()
        sends.append(c)
    total = x_ref[piece(row), :]
    for s in range(1, rows_n):
        sends[s - 1].wait_recv()
        total = total + inbox[s - 1]
    out_ref[piece(row), :] = total
    back = []
    for s in range(1, rows_n):
        c = pltpu.make_async_remote_copy(
            src_ref=out_ref.at[piece(row)],
            dst_ref=out_ref.at[piece(row)],
            send_sem=b_send.at[s - 1],
            recv_sem=b_recv.at[s - 1],
            device_id={"row": lax.rem(row + s, rows_n)},
            device_id_type=MESH,
        )
        c.start()
        back.append(c)
    for c in sends:
        c.wait_send()
    for c in back:
        c.wait()


def sum_rows(x, rows_n):
    dma = pltpu.SemaphoreType.DMA
    return pl.pallas_call(
        functools.partial(reduce_kernel, rows_n),
        out_shape=jax.ShapeDtypeStruct(x.shape, x.dtype),
        in_specs=[pl.BlockSpec(memory_space=pltpu.VMEM)],
        out_specs=pl.BlockSpec(memory_space=pltpu.VMEM),
        scratch_shapes=[pltpu.VMEM((rows_n - 1, x.shape[0] // rows_n, x.shape[1]), x.dtype)]
        + [dma((rows_n - 1,))] * 4,
        compiler_params=pltpu.CompilerParams(
            collective_id=2, has_side_effects=True, vmem_limit_bytes=24 * 2**20
        ),
    )(x)


def on_device(
    root_inverse,
    root_factor_one,
    diag_inverse_one,
    root_factor_two,
    parent_factor,
    diag_inverse_two,
    root_mask_one,
    root_mask_two,
    parents,
    row_count,
):
    width = parent_factor.shape[1]
    local_rows = root_inverse.shape[0]
    per_one = diag_inverse_one.shape[0]
    per_two = diag_inverse_two.shape[0]
    row_index = lax.axis_index("row")
    col_index = lax.axis_index("col")
    blocks = local_rows // width

    def row_masks(mask, number):
        own = lax.dynamic_slice(mask, (col_index * number, row_index * blocks), (number, blocks))
        return jnp.repeat(own.T.astype(jnp.float32), width, axis=0)

    mask_one = row_masks(root_mask_one, per_one)
    mask_two = row_masks(root_mask_two, per_two)
    one = [
        root_factor_one[:, k * width : (k + 1) * width] * mask_one[:, k : k + 1]
        for k in range(per_one)
    ]
    two = [
        root_factor_two[:, k * width : (k + 1) * width] * mask_two[:, k : k + 1]
        for k in range(per_two)
    ]
    half = width // 2
    early = jnp.concatenate(one + [two[0][:, :half]], axis=1)
    panel = lax.all_gather(root_inverse, "col", axis=1, tiled=True)
    whole_early = gather_first(early, row_count, 0)
    late = jnp.concatenate([two[0][:, half:]] + two[1:], axis=1)
    whole_one = [whole_early[:, k * width : (k + 1) * width] for k in range(per_one)]

    def dot(a, b):
        return jnp.dot(a, b, precision=HIGH, preferred_element_type=jnp.float32)

    def dot_t(a, b):
        return lax.dot_general(
            a, b, (((0,), (0,)), ((), ())), precision=HIGH, preferred_element_type=jnp.float32
        )

    inv_one = [-dot(panel, whole_one[k]) * mask_one[:, k : k + 1] for k in range(per_one)]
    inverse_one = jnp.concatenate(inv_one, axis=1) if per_one > 1 else inv_one[0]
    first = row_index == 0
    excess = [
        dot_t(one[k], inv_one[k]) - jnp.where(first, diag_inverse_one[k], 0.0)
        for k in range(per_one)
    ]
    own_parents = lax.dynamic_slice_in_dim(parents, col_index * per_two, per_two, 0)
    stacked = jnp.concatenate([inverse_one, jnp.concatenate(excess, axis=1)], axis=0)
    stacked, late = lax.optimization_barrier((stacked, late))
    everyone = lax.all_gather(stacked, "col", axis=0, tiled=False)
    whole_late = gather_first(late, row_count, 1)
    everyone, whole_late = lax.optimization_barrier((everyone, whole_late))
    parent_cols, parent_part = [], []
    for k in range(per_two):
        p = own_parents[k]
        own = lax.dynamic_slice(
            everyone,
            (p // per_one, jnp.int32(0), (p % per_one) * width),
            (1, local_rows + width, width),
        )[0]
        parent_cols.append(own[:local_rows])
        parent_part.append(
            dot_t(own[:local_rows], two[k]) - dot(own[local_rows:], parent_factor[k])
        )
    cross = [dot(parent_cols[k], parent_factor[k]) for k in range(per_two)]
    inner = [dot_t(parent_factor[k], parent_part[k]) for k in range(per_two)]
    inv_two = []
    for k in range(per_two):
        if k == 0:
            whole = jnp.concatenate(
                [whole_early[:, per_one * width :], whole_late[:, :half]], axis=1
            )
        else:
            whole = whole_late[:, half + (k - 1) * width : half + k * width]
        inv_two.append(-(dot(panel, whole) + cross[k]) * mask_two[:, k : k + 1])
    diag_part_two = [dot_t(two[k], inv_two[k]) - inner[k] for k in range(per_two)]
    sums = sum_rows(jnp.concatenate(excess + parent_part + diag_part_two, axis=0), row_count)
    sums = sums.reshape(per_one + 2 * per_two, width, width)
    diag_one = -sums[:per_one]
    summed_parent = sums[per_one : per_one + per_two]
    diag_two = diag_inverse_two - sums[per_one + per_two :]
    return (
        inverse_one,
        diag_one,
        jnp.concatenate(inv_two, axis=1),
        -summed_parent,
        diag_two,
    )


def solution(mesh):
    row_count = mesh.shape["row"]
    tall = P(("pole", "row"), "col")
    deep = P(("pole", "col"), None, None)

    def step(*args):
        return on_device(*args, row_count)

    return jax.shard_map(
        step,
        mesh=mesh,
        in_specs=(tall, tall, deep, tall, deep, deep, P(), P(), P()),
        out_specs=(tall, deep, tall, deep, deep),
        check_vma=False,
    )
```

```python
import functools

import jax
import jax.numpy as jnp
from jax import lax
from jax.experimental import pallas as pl
from jax.experimental.pallas import tpu as pltpu
from jax.sharding import PartitionSpec as P

HIGH = lax.Precision.HIGH


MESH = pl.DeviceIdType.MESH


def gather_kernel(rows_n, f_ref, whole, f_send, f_recv, own):
    row = lax.axis_index("row")
    tall = f_ref.shape[0]
    barrier = pltpu.get_barrier_semaphore()
    for s in range(1, rows_n):
        pl.semaphore_signal(
            barrier, inc=1, device_id={"row": lax.rem(row + s, rows_n)}, device_id_type=MESH
        )
    pl.semaphore_wait(barrier, rows_n - 1)
    place = whole.at[pl.ds(pl.multiple_of(row * tall, tall), tall)]
    sends = []
    for s in range(1, rows_n):
        c = pltpu.make_async_remote_copy(
            src_ref=f_ref,
            dst_ref=place,
            send_sem=f_send.at[s - 1],
            recv_sem=f_recv.at[s - 1],
            device_id={"row": lax.rem(row + s, rows_n)},
            device_id_type=MESH,
        )
        c.start()
        sends.append(c)
    local = pltpu.make_async_copy(f_ref, place, own)
    local.start()
    for c in sends:
        c.wait()
    local.wait()


def gather_first(f, rows_n, number):
    dma = pltpu.SemaphoreType.DMA
    return pl.pallas_call(
        functools.partial(gather_kernel, rows_n),
        out_shape=jax.ShapeDtypeStruct((rows_n * f.shape[0], f.shape[1]), f.dtype),
        in_specs=[pl.BlockSpec(memory_space=pl.ANY)],
        out_specs=pl.BlockSpec(memory_space=pl.ANY),
        scratch_shapes=[dma((rows_n - 1,)), dma((rows_n - 1,)), dma],
        compiler_params=pltpu.CompilerParams(collective_id=number, has_side_effects=True),
    )(f)


def reduce_kernel(rows_n, x_ref, out_ref, inbox, a_send, a_recv, b_send, b_recv):
    row = lax.axis_index("row")
    part = x_ref.shape[0] // rows_n
    barrier = pltpu.get_barrier_semaphore()
    for s in range(1, rows_n):
        pl.semaphore_signal(
            barrier, inc=1, device_id={"row": lax.rem(row + s, rows_n)}, device_id_type=MESH
        )
    pl.semaphore_wait(barrier, rows_n - 1)

    half = part // 2

    def piece(r, h):
        return pl.ds(pl.multiple_of(r * part + h * half, half), half)

    def there(s, h):
        other = lax.rem(row + s, rows_n)
        return pltpu.make_async_remote_copy(
            src_ref=x_ref.at[piece(other, h)],
            dst_ref=inbox.at[h, s - 1],
            send_sem=a_send.at[h, s - 1],
            recv_sem=a_recv.at[h, s - 1],
            device_id={"row": other},
            device_id_type=MESH,
        )

    def back(s, h):
        return pltpu.make_async_remote_copy(
            src_ref=out_ref.at[piece(row, h)],
            dst_ref=out_ref.at[piece(row, h)],
            send_sem=b_send.at[h, s - 1],
            recv_sem=b_recv.at[h, s - 1],
            device_id={"row": lax.rem(row + s, rows_n)},
            device_id_type=MESH,
        )

    pairs = [(s, h) for h in range(2) for s in range(1, rows_n)]
    for s, h in pairs:
        there(s, h).start()
    for h in range(2):
        total = x_ref[piece(row, h), :]
        for s in range(1, rows_n):
            there(s, h).wait_recv()
            total = total + inbox[h, s - 1]
        out_ref[piece(row, h), :] = total
        for s in range(1, rows_n):
            back(s, h).start()
    for s, h in pairs:
        there(s, h).wait_send()
        back(s, h).wait()


def sum_rows(x, rows_n):
    dma = pltpu.SemaphoreType.DMA
    return pl.pallas_call(
        functools.partial(reduce_kernel, rows_n),
        out_shape=jax.ShapeDtypeStruct(x.shape, x.dtype),
        in_specs=[pl.BlockSpec(memory_space=pltpu.VMEM)],
        out_specs=pl.BlockSpec(memory_space=pltpu.VMEM),
        scratch_shapes=[pltpu.VMEM((2, rows_n - 1, x.shape[0] // rows_n // 2, x.shape[1]), x.dtype)]
        + [dma((2, rows_n - 1))] * 4,
        compiler_params=pltpu.CompilerParams(
            collective_id=2, has_side_effects=True, vmem_limit_bytes=24 * 2**20
        ),
    )(x)


def on_device(
    root_inverse,
    root_factor_one,
    diag_inverse_one,
    root_factor_two,
    parent_factor,
    diag_inverse_two,
    root_mask_one,
    root_mask_two,
    parents,
    row_count,
):
    width = parent_factor.shape[1]
    local_rows = root_inverse.shape[0]
    per_one = diag_inverse_one.shape[0]
    per_two = diag_inverse_two.shape[0]
    row_index = lax.axis_index("row")
    col_index = lax.axis_index("col")
    blocks = local_rows // width

    def row_masks(mask, number):
        own = lax.dynamic_slice(mask, (col_index * number, row_index * blocks), (number, blocks))
        return jnp.repeat(own.T.astype(jnp.float32), width, axis=0)

    mask_one = row_masks(root_mask_one, per_one)
    mask_two = row_masks(root_mask_two, per_two)
    one = [
        root_factor_one[:, k * width : (k + 1) * width] * mask_one[:, k : k + 1]
        for k in range(per_one)
    ]
    two = [
        root_factor_two[:, k * width : (k + 1) * width] * mask_two[:, k : k + 1]
        for k in range(per_two)
    ]
    half = width // 2
    early = jnp.concatenate(one + [two[0][:, :half]], axis=1)
    panel = lax.all_gather(root_inverse, "col", axis=1, tiled=True)
    whole_early = gather_first(early, row_count, 0)
    late = jnp.concatenate([two[0][:, half:]] + two[1:], axis=1)
    whole_one = [whole_early[:, k * width : (k + 1) * width] for k in range(per_one)]

    def dot(a, b):
        return jnp.dot(a, b, precision=HIGH, preferred_element_type=jnp.float32)

    def dot_t(a, b):
        return lax.dot_general(
            a, b, (((0,), (0,)), ((), ())), precision=HIGH, preferred_element_type=jnp.float32
        )

    inv_one = [-dot(panel, whole_one[k]) * mask_one[:, k : k + 1] for k in range(per_one)]
    inverse_one = jnp.concatenate(inv_one, axis=1) if per_one > 1 else inv_one[0]
    first = row_index == 0
    excess = [
        dot_t(one[k], inv_one[k]) - jnp.where(first, diag_inverse_one[k], 0.0)
        for k in range(per_one)
    ]
    own_parents = lax.dynamic_slice_in_dim(parents, col_index * per_two, per_two, 0)
    stacked = jnp.concatenate([inverse_one, jnp.concatenate(excess, axis=1)], axis=0)
    stacked, late = lax.optimization_barrier((stacked, late))
    everyone = lax.all_gather(stacked, "col", axis=0, tiled=True)
    whole_late = gather_first(late, row_count, 1)
    everyone, whole_late = lax.optimization_barrier((everyone, whole_late))
    parent_cols, parent_part = [], []
    for k in range(per_two):
        p = own_parents[k]
        own = lax.dynamic_slice(
            everyone,
            ((p // per_one) * (local_rows + width), (p % per_one) * width),
            (local_rows + width, width),
        )
        parent_cols.append(own[:local_rows])
        parent_part.append(
            dot_t(own[:local_rows], two[k]) - dot(own[local_rows:], parent_factor[k])
        )
    cross = [dot(parent_cols[k], parent_factor[k]) for k in range(per_two)]
    inner = [dot_t(parent_factor[k], parent_part[k]) for k in range(per_two)]
    inv_two = []
    for k in range(per_two):
        if k == 0:
            whole = jnp.concatenate(
                [whole_early[:, per_one * width :], whole_late[:, :half]], axis=1
            )
        else:
            whole = whole_late[:, half + (k - 1) * width : half + k * width]
        inv_two.append(-(dot(panel, whole) + cross[k]) * mask_two[:, k : k + 1])
    diag_part_two = [dot_t(two[k], inv_two[k]) - inner[k] for k in range(per_two)]
    sums = sum_rows(jnp.concatenate(excess + parent_part + diag_part_two, axis=0), row_count)
    sums = sums.reshape(per_one + 2 * per_two, width, width)
    diag_one = -sums[:per_one]
    summed_parent = sums[per_one : per_one + per_two]
    diag_two = diag_inverse_two - sums[per_one + per_two :]
    return (
        inverse_one,
        diag_one,
        jnp.concatenate(inv_two, axis=1),
        -summed_parent,
        diag_two,
    )


def solution(mesh):
    row_count = mesh.shape["row"]
    tall = P(("pole", "row"), "col")
    deep = P(("pole", "col"), None, None)

    def step(*args):
        return on_device(*args, row_count)

    return jax.shard_map(
        step,
        mesh=mesh,
        in_specs=(tall, tall, deep, tall, deep, deep, P(), P(), P()),
        out_specs=(tall, deep, tall, deep, deep),
        check_vma=False,
    )
```
